512 devices in a mesh: dp: 16 (over y, core), ctx: 32 (over x, z).
Axes of the slice: x: 4, y: 8, z: 8, core: 2. Of those that a mesh axis runs over, the one named last changes fastest.
Arguments:
- queries: bfloat16 [16, 4096, 4096], P('dp', 'ctx'), may hold values from -45 to 45
- key_head_states: bfloat16 [16, 4096, 512], P('dp', 'ctx'), may hold values from -6 to 6
- value_head_states: bfloat16 [16, 4096, 512], P('dp', 'ctx'), may hold values from -6 to 6
- out_grad: bfloat16 [16, 4096, 4096], P('dp', 'ctx'), may hold values from -24 to 24
- doc_blocks: int32 [16, 21], P('dp'), may hold values from 1 to 8, as said below
- block_order: int32 [16, 64], P('dp'), may hold values from 0 to 63, as said below
- target_mask: int32 [16, 4096], P('dp', 'ctx'), may hold values from 0 to 1, as said below
Outputs:
- attended: bfloat16 [16, 4096, 4096], P('dp', 'ctx')
- grad_queries: bfloat16 [16, 4096, 4096], P('dp', 'ctx')
- grad_keys: bfloat16 [16, 4096, 512], P('dp', 'ctx')
- grad_values: bfloat16 [16, 4096, 512], P('dp', 'ctx')
The draws below stay inside these ranges and needn't reach their ends.
Inputs may be any that keep to these rules, and one draw needn't show every extreme that they name: `doc_blocks`: each pack's lengths sum to 64; the longest is 8. `block_order`: each pack's row is a permutation of its blocks that stores the blocks of every document next to one another and in pack order. `target_mask`: the first token of every stored block is 1.
All inputs are finite; a program needn't handle non-finite values.
Results may differ from the reference program's by a relative error of at most 0.03.
Values may be sent and summed in bfloat16 or wider, within the bound.
No kernel may reach another device: no remote copies, remote signals or barrier semaphores. Data moves between devices by JAX's collectives and lax.ppermute only.
A program may use at most 64 MiB of HBM per device.

```python
import math
import jax
import jax.numpy as jnp
from jax import lax

HEAD_WIDTH = 128
QUERY_HEADS = 32
KEY_VALUE_HEADS = 4
ALIGN_TOKENS = 64
MOST = 8
TOK_DEV = 128
PACK_TOTAL = 16
PACK_TOKENS = 4096
BLOCKS = 64
NDOCS = 21


def pack_layout(pack_key):
    others = NDOCS - 1
    room = MOST - 1
    extra = BLOCKS - NDOCS - room
    doc_ids = jnp.arange(NDOCS, dtype=jnp.int32)
    long_doc = jax.random.randint(jax.random.fold_in(pack_key, 1), (), 0, NDOCS)
    ranks = jax.random.permutation(jax.random.fold_in(pack_key, 2), others * room)
    taken = jnp.sum((ranks < extra).astype(jnp.int32).reshape(others, room), axis=1)
    other_index = doc_ids - (doc_ids > long_doc).astype(jnp.int32)
    picked = (other_index[:, None] == jnp.arange(others, dtype=jnp.int32)[None, :]).astype(jnp.int32)
    counts = jnp.sum(picked * taken[None, :], axis=1)
    lengths = 1 + jnp.where(doc_ids == long_doc, room, counts)
    place = jax.random.permutation(jax.random.fold_in(pack_key, 3), NDOCS)
    pack_start = jnp.cumsum(lengths) - lengths
    which = (place[:, None] == doc_ids[None, :]).astype(jnp.int32)
    stored_len = jnp.sum(which * lengths[None, :], axis=1)
    stored_start = jnp.cumsum(stored_len) - stored_len
    source_start = jnp.sum(which * pack_start[None, :], axis=1)
    block_ids = jnp.arange(BLOCKS, dtype=jnp.int32)
    slot = jnp.sum((block_ids[:, None] >= (stored_start + stored_len)[None, :]).astype(jnp.int32), axis=1)
    in_slot = (slot[:, None] == doc_ids[None, :]).astype(jnp.int32)
    order_row = jnp.sum(in_slot * (source_start - stored_start)[None, :], axis=1) + block_ids
    return (lengths.astype(jnp.int32), order_row.astype(jnp.int32))


def layouts(key):
    pack_ids = jnp.arange(PACK_TOTAL, dtype=jnp.int32)
    return jax.vmap(lambda index: pack_layout(jax.random.fold_in(key, index + 1000)))(pack_ids)


def draw_doc_blocks(key, part):
    lengths, order_rows = layouts(key)
    return lengths


def draw_block_order(key, part):
    lengths, order_rows = layouts(key)
    return order_rows


def draw_key_head_states(key, part):
    key = jax.random.fold_in(key, 3)
    score_grid_shape = (PACK_TOTAL, PACK_TOKENS, KEY_VALUE_HEADS, HEAD_WIDTH)
    score_grid = jnp.clip(jax.random.normal(key, score_grid_shape), -6.0, 6.0)
    return score_grid.reshape(PACK_TOTAL, PACK_TOKENS, KEY_VALUE_HEADS * HEAD_WIDTH).astype(jnp.bfloat16)


def draw_queries(key, part):
    key = jax.random.fold_in(key, 5)
    score_grid = jnp.clip(jax.random.normal(key, (PACK_TOTAL, PACK_TOKENS, QUERY_HEADS * HEAD_WIDTH)), -6.0, 6.0)
    return score_grid.reshape(PACK_TOTAL, PACK_TOKENS, QUERY_HEADS * HEAD_WIDTH).astype(jnp.bfloat16)


def draw_target_mask(key, part):
    key = jax.random.fold_in(key, 17)
    row_numbers = lax.broadcasted_iota(jnp.int32, (PACK_TOTAL, PACK_TOKENS), 1)
    pack_ids = lax.broadcasted_iota(jnp.int32, (PACK_TOTAL, PACK_TOKENS), 0)
    shard_count = PACK_TOTAL * (PACK_TOKENS // TOK_DEV)
    place = pack_ids * (PACK_TOKENS // TOK_DEV) + row_numbers // TOK_DEV
    level = 200 + 600 * place // max(shard_count - 1, 1)
    ticket = jax.random.randint(key, (PACK_TOTAL, PACK_TOKENS), 0, 1000)
    return jnp.where((ticket < level) | (row_numbers % ALIGN_TOKENS == 0), 1, 0).astype(jnp.int32)


def shard_levels(rng, shape, cuts, smallest, top_value):
    gain = 1.0
    for dim, blocks in cuts:
        steps = jax.random.uniform(jax.random.fold_in(jax.random.fold_in(rng, 6), dim), (blocks,), jnp.float32, smallest / len(cuts), top_value / len(cuts))
        gain = gain * jnp.repeat(jnp.exp(steps), shape[dim] // blocks).reshape((-1,) + (1,) * (len(shape) - 1 - dim))
    return gain


def centred(key, shape, width, limit, cuts=(), kind=jnp.bfloat16):
    loudness = shard_levels(key, shape, cuts, -0.22, 0.18) if cuts else 1.0
    array = jax.random.normal(key, shape, jnp.float32) * width * loudness
    return jnp.minimum(jnp.maximum(array, -limit), limit).astype(kind)


def setup_inputs(seed: int = 0) -> dict:
    arg_keys = jax.random.split(jax.random.key(seed), 8)
    return {
        "queries": draw_queries(jax.random.fold_in(arg_keys[7], 71), 0),
        "key_head_states": draw_key_head_states(jax.random.fold_in(arg_keys[7], 71), 0),
        "value_head_states": centred(arg_keys[2], (PACK_TOTAL, PACK_TOKENS, KEY_VALUE_HEADS * HEAD_WIDTH), 1.0, 6.0, ((0, 16), (1, 32))),
        "out_grad": centred(arg_keys[3], (PACK_TOTAL, PACK_TOKENS, QUERY_HEADS * HEAD_WIDTH), 4.0, 24.0, ((0, 16), (1, 32))),
        "doc_blocks": draw_doc_blocks(jax.random.fold_in(arg_keys[7], 71), 0),
        "block_order": draw_block_order(jax.random.fold_in(arg_keys[7], 71), 0),
        "target_mask": draw_target_mask(jax.random.fold_in(arg_keys[7], 71), 0),
    }


def block_documents(doc_lengths, block_count, block_size):
    ends = jnp.cumsum(doc_lengths, dtype=jnp.int32)
    block_ids = jnp.arange(block_count, dtype=jnp.int32)
    owners = lax.optimization_barrier(jnp.sum((block_ids[:, None] >= ends[None, :]).astype(jnp.int32), axis=1))
    return jnp.repeat(owners, block_size)

def token_permute(stored, positions, block_size):
    pieces = stored.reshape((stored.shape[0] // block_size, block_size) + stored.shape[1:])
    return jnp.take(pieces, positions, axis=0).reshape(stored.shape)

def band_pass(queries, key_head_states, value_head_states, grads, documents, span):
    pack_rows, head_count, head_size = queries.shape
    inv_scale = 1.0 / math.sqrt(head_size)
    row_numbers = jnp.arange(span, dtype=jnp.int32)
    col_ids = jnp.arange(2 * span, dtype=jnp.int32)

    def step(carry, step_index):
        acc_keys, acc_values = carry
        q_start = step_index * span
        k_start = jnp.maximum(step_index - 1, 0) * span
        q_block = lax.dynamic_slice_in_dim(queries, q_start, span, 0)
        g_block = lax.dynamic_slice_in_dim(grads, q_start, span, 0)
        k_window = lax.dynamic_slice_in_dim(key_head_states, k_start, 2 * span, 0)
        v_window = lax.dynamic_slice_in_dim(value_head_states, k_start, 2 * span, 0)
        q_docs = lax.dynamic_slice_in_dim(documents, q_start, span, 0)
        k_docs = lax.dynamic_slice_in_dim(documents, k_start, 2 * span, 0)
        visible = (q_docs[:, None] == k_docs[None, :]) & (k_start + col_ids[None, :] <= q_start + row_numbers[:, None])
        scores = jnp.einsum('qhd,khd->hqk', q_block.astype(jnp.float32), k_window.astype(jnp.float32)) * inv_scale
        scores = jnp.where(visible[None], scores, -1e+30)
        peak = lax.optimization_barrier(jnp.max(scores, axis=2, keepdims=True))
        expo = jnp.exp(scores - peak)
        prob_high = expo / lax.optimization_barrier(jnp.sum(expo, axis=2, keepdims=True))
        prob_low = prob_high.astype(jnp.bfloat16)
        out_block = jnp.einsum('hqk,khd->qhd', prob_low.astype(jnp.float32), v_window.astype(jnp.float32)).astype(jnp.bfloat16)
        delta = lax.optimization_barrier(jnp.sum(g_block.astype(jnp.float32) * out_block.astype(jnp.float32), axis=2))
        dprob = jnp.einsum('qhd,khd->hqk', g_block.astype(jnp.float32), v_window.astype(jnp.float32))
        dscore = (prob_high * (dprob - jnp.transpose(delta)[:, :, None]) * inv_scale).astype(jnp.bfloat16)
        dq_block = jnp.einsum('hqk,khd->qhd', dscore.astype(jnp.float32), k_window.astype(jnp.float32)).astype(jnp.bfloat16)
        key_part = jnp.einsum('hqk,qhd->khd', dscore.astype(jnp.float32), q_block.astype(jnp.float32))
        value_part = jnp.einsum('hqk,qhd->khd', prob_low.astype(jnp.float32), g_block.astype(jnp.float32))
        acc_keys = lax.dynamic_update_slice_in_dim(acc_keys, lax.dynamic_slice_in_dim(acc_keys, k_start, 2 * span, 0) + key_part, k_start, 0)
        acc_values = lax.dynamic_update_slice_in_dim(acc_values, lax.dynamic_slice_in_dim(acc_values, k_start, 2 * span, 0) + value_part, k_start, 0)
        return ((acc_keys, acc_values), (out_block, dq_block))
    zeros_acc = jnp.zeros((pack_rows, head_count, head_size), jnp.float32)
    (acc_keys, acc_values), (out_blocks, dq_blocks) = lax.scan(step, (zeros_acc, zeros_acc), jnp.arange(pack_rows // span, dtype=jnp.int32))
    attention_output = out_blocks.reshape(pack_rows, head_count, head_size)
    query_gradient = dq_blocks.reshape(pack_rows, head_count, head_size)
    return (attention_output, query_gradient, acc_keys, acc_values)

def reference(queries, key_head_states, value_head_states, out_grad, doc_blocks, block_order, target_mask):
    target_total = jnp.sum(target_mask.astype(jnp.float32))
    factor = PACK_TOTAL * PACK_TOKENS / target_total
    query_per_group = QUERY_HEADS // KEY_VALUE_HEADS
    span = MOST * ALIGN_TOKENS

    def one_pack(items):
        pack_queries, packed_key_rows, packed_value_rows, pack_grad, lengths, positioned, mask_row = items
        grads = (pack_grad.astype(jnp.float32) * (mask_row.astype(jnp.float32)[:, None] * factor)).astype(jnp.bfloat16)
        inverse_permute = jnp.zeros((BLOCKS,), jnp.int32).at[positioned].set(jnp.arange(BLOCKS, dtype=jnp.int32))
        documents = block_documents(lengths, BLOCKS, ALIGN_TOKENS)
        q_true = token_permute(pack_queries, inverse_permute, ALIGN_TOKENS).reshape(PACK_TOKENS, QUERY_HEADS, HEAD_WIDTH)
        exact_keys = jnp.repeat(token_permute(packed_key_rows, inverse_permute, ALIGN_TOKENS).reshape(PACK_TOKENS, KEY_VALUE_HEADS, HEAD_WIDTH), query_per_group, axis=1)
        exact_values = jnp.repeat(token_permute(packed_value_rows, inverse_permute, ALIGN_TOKENS).reshape(PACK_TOKENS, KEY_VALUE_HEADS, HEAD_WIDTH), query_per_group, axis=1)
        g_true = token_permute(grads, inverse_permute, ALIGN_TOKENS).reshape(PACK_TOKENS, QUERY_HEADS, HEAD_WIDTH)
        attention_output, query_gradient, key_gradient_terms, value_gradient_terms = band_pass(q_true, exact_keys, exact_values, g_true, documents, span)
        key_gradient = lax.optimization_barrier(jnp.sum(key_gradient_terms.reshape(PACK_TOKENS, KEY_VALUE_HEADS, query_per_group, HEAD_WIDTH), axis=2)).astype(jnp.bfloat16)
        value_gradient = lax.optimization_barrier(jnp.sum(value_gradient_terms.reshape(PACK_TOKENS, KEY_VALUE_HEADS, query_per_group, HEAD_WIDTH), axis=2)).astype(jnp.bfloat16)
        return (token_permute(attention_output.reshape(PACK_TOKENS, QUERY_HEADS * HEAD_WIDTH), positioned, ALIGN_TOKENS), token_permute(query_gradient.reshape(PACK_TOKENS, QUERY_HEADS * HEAD_WIDTH), positioned, ALIGN_TOKENS), token_permute(key_gradient.reshape(PACK_TOKENS, KEY_VALUE_HEADS * HEAD_WIDTH), positioned, ALIGN_TOKENS), token_permute(value_gradient.reshape(PACK_TOKENS, KEY_VALUE_HEADS * HEAD_WIDTH), positioned, ALIGN_TOKENS))
    attended, grad_queries, grad_keys, grad_values = lax.map(one_pack, (queries, key_head_states, value_head_states, out_grad, doc_blocks, block_order, target_mask))
    return (attended, grad_queries, grad_keys, grad_values)
```

```python
import math

import jax
import jax.numpy as jnp
from jax import lax
from jax.experimental import pallas as pl
from jax.experimental.pallas import tpu as pltpu
from jax.sharding import PartitionSpec as P

HEAD_WIDTH = 128
QUERY_HEADS = 32
KEY_VALUE_HEADS = 4
ALIGN_TOKENS = 64
MOST = 8
GROUP = QUERY_HEADS // KEY_VALUE_HEADS
SPAN = MOST * ALIGN_TOKENS
LOG2E = math.log2(math.e)
SCALE = 1.0 / math.sqrt(HEAD_WIDTH)
HIDDEN = -1e30
CHUNK_HEADS = 4


def dot_nt(a, b):
    return lax.dot_general(a, b, (((1,), (1,)), ((), ())), preferred_element_type=jnp.float32)


def dot_nn(a, b):
    return lax.dot_general(a, b, (((1,), (0,)), ((), ())), preferred_element_type=jnp.float32)


def attention_kernel(
    back_ref,
    q_ref,
    g_ref,
    own_ref,
    near_ref,
    mid_ref,
    far_ref,
    last_ref,
    out_ref,
    dq_ref,
    own_part,
    near_part,
    mid_part,
    far_part,
    last_part,
    acc_ref,
):
    width = HEAD_WIDTH
    block = ALIGN_TOKENS
    window = jnp.concatenate(
        [last_ref[...], far_ref[...], mid_ref[...], near_ref[...], own_ref[...]], axis=0
    )
    keys, values = window[:, :width], window[:, width:]
    keys_t, values_t = jnp.transpose(keys), jnp.transpose(values)
    cols = CHUNK_HEADS * block
    causal = lax.broadcasted_iota(jnp.int32, (block, cols), 0) <= (
        lax.broadcasted_iota(jnp.int32, (block, cols), 1) & (block - 1)
    )
    rows = window.shape[0]
    acc_ref[SPAN:rows, :] = jnp.zeros((rows - SPAN, 2 * width), jnp.float32)
    for t in range(rows // block - MOST + 1):
        lo = t * block
        back = back_ref[t]
        k_t, v_t = keys[lo : lo + SPAN], values[lo : lo + SPAN]
        kt_t, vt_t = keys_t[:, lo : lo + SPAN], values_t[:, lo : lo + SPAN]
        dk = dv = None
        for c in range(GROUP // CHUNK_HEADS):
            heads = range(c * CHUNK_HEADS, (c + 1) * CHUNK_HEADS)
            q = jnp.concatenate(
                [q_ref[lo : lo + block, h * width : (h + 1) * width] for h in heads], axis=0
            )
            g = jnp.concatenate(
                [g_ref[lo : lo + block, h * width : (h + 1) * width] for h in heads], axis=0
            )
            s = dot_nt(k_t, q)
            dp = dot_nt(v_t, g)
            parts = [
                s[b * block : (b + 1) * block] + jnp.where(b >= MOST - 1 - back, 0.0, HIDDEN)
                for b in range(MOST - 1)
            ]
            parts.append(jnp.where(causal, s[SPAN - block :], HIDDEN))
            s = jnp.concatenate(parts, axis=0)
            peak = jnp.max(s, axis=0, keepdims=True)
            e = jnp.exp2((s - peak) * (SCALE * LOG2E))
            p = e * (1.0 / jnp.sum(e, axis=0, keepdims=True))
            p_low = p.astype(jnp.bfloat16)
            delta = jnp.sum(p * dp, axis=0, keepdims=True)
            ds = (p * (dp - delta)).astype(jnp.bfloat16)
            dk_c, dv_c = dot_nn(ds, q), dot_nn(p_low, g)
            dk, dv = (dk_c, dv_c) if dk is None else (dk + dk_c, dv + dv_c)
            out_c = jnp.transpose(dot_nn(vt_t, p_low)).astype(jnp.bfloat16)
            dq_c = jnp.transpose(dot_nn(kt_t, ds) * SCALE).astype(jnp.bfloat16)
            for i, h in enumerate(heads):
                at = (slice(lo, lo + block), slice(h * width, (h + 1) * width))
                out_ref[at] = out_c[i * block : (i + 1) * block]
                dq_ref[at] = dq_c[i * block : (i + 1) * block]
        part = jnp.concatenate([dk * SCALE, dv], axis=1)
        if t == 0:
            acc_ref[0:SPAN, :] = part
        else:
            acc_ref[lo : lo + SPAN, :] = acc_ref[lo : lo + SPAN, :] + part
    at = 0
    for ref in (last_part, far_part, mid_part, near_part, own_part):
        ref[...] = acc_ref[at : at + ref.shape[0], :].astype(ref.dtype)
        at += ref.shape[0]


def attention(back, queries, grads, own, near, mid, far, last):
    tokens = queries.shape[0]
    tail = last.shape[0]
    columns = lambda n, w: pl.BlockSpec((n, w), lambda i, *_: (0, i))
    pair = 2 * HEAD_WIDTH
    wide = GROUP * HEAD_WIDTH
    kv_specs = [columns(tokens, pair)] * 4 + [columns(tail, pair)]
    shape = jax.ShapeDtypeStruct
    return pl.pallas_call(
        attention_kernel,
        grid_spec=pltpu.PrefetchScalarGridSpec(
            num_scalar_prefetch=1,
            grid=(KEY_VALUE_HEADS,),
            in_specs=[columns(tokens, wide)] * 2 + kv_specs,
            out_specs=[columns(tokens, wide)] * 2 + kv_specs,
            scratch_shapes=[pltpu.VMEM((4 * tokens + tail, pair), jnp.float32)],
        ),
        out_shape=[
            shape(queries.shape, jnp.bfloat16),
            shape(queries.shape, jnp.bfloat16),
            shape(own.shape, jnp.float32),
            shape(own.shape, jnp.bfloat16),
            shape(own.shape, jnp.bfloat16),
            shape(own.shape, jnp.bfloat16),
            shape(last.shape, jnp.bfloat16),
        ],
        compiler_params=pltpu.CompilerParams(vmem_limit_bytes=48 * 1024 * 1024),
        name="attention",
    )(back, queries, grads, own, near, mid, far, last)


def blocks_back(lengths, order, first, count):
    ends = jnp.sum(
        jnp.where(
            jnp.arange(lengths.shape[0])[:, None] >= jnp.arange(lengths.shape[0])[None, :],
            lengths[None, :],
            0,
        ),
        axis=1,
    )
    places = lax.dynamic_slice_in_dim(order, first, count, 0)
    starts = jnp.max(jnp.where(ends[None, :] <= places[:, None], ends[None, :], 0), axis=1)
    return places - starts


def count_ones(target_mask):
    local = jnp.sum(target_mask.astype(jnp.float32))
    total = local
    for axis in ("dp", "ctx"):
        n = lax.axis_size(axis)
        sent = jnp.broadcast_to(total, (n, 1, 128))
        total = jnp.sum(lax.all_to_all(sent, axis, split_axis=0, concat_axis=0)[:, 0, 0])
    return total


def shards(
    queries, key_head_states, value_head_states, out_grad, doc_blocks, block_order, target_mask
):
    tokens = queries.shape[1]
    ctx_count = lax.axis_size("ctx")
    pack_rows = tokens * ctx_count
    heads, width = KEY_VALUE_HEADS, HEAD_WIDTH

    def shift(array, steps):
        pairs = [
            (i, i + steps) for i in range(ctx_count) if 0 <= i + steps < ctx_count
        ]
        return lax.ppermute(array, "ctx", pairs)

    own = jnp.concatenate(
        [
            key_head_states.reshape(tokens, heads, 1, width),
            value_head_states.reshape(tokens, heads, 1, width),
        ],
        axis=2,
    ).reshape(tokens, 2 * heads * width)
    tail = SPAN - ALIGN_TOKENS - 3 * tokens
    far_to_near = [
        shift(own[tokens - tail :], 4),
        shift(own, 3),
        shift(own, 2),
        shift(own, 1),
    ]
    last, far, mid, near = far_to_near
    total = count_ones(target_mask)
    factor = lax.axis_size("dp") * pack_rows / total
    grads = out_grad[0] * target_mask[0].astype(jnp.bfloat16)[:, None]
    blocks = tokens // ALIGN_TOKENS
    back = blocks_back(
        doc_blocks[0], block_order[0], lax.axis_index("ctx") * blocks, blocks
    )
    attended, dq, own_part, near_part, mid_part, far_part, last_part = attention(
        back, queries[0], grads, own, near, mid, far, last
    )
    last_back = shift(last_part, -4)
    far_back = shift(far_part, -3)
    mid_back = shift(mid_part, -2)
    near_back = shift(near_part, -1)
    grad_queries = (dq.astype(jnp.float32) * factor).astype(jnp.bfloat16)
    whole = own_part
    for part in (near_back, mid_back, far_back):
        whole = whole + part.astype(jnp.float32)
    whole = whole + jnp.pad(last_back.astype(jnp.float32), ((tokens - tail, 0), (0, 0)))
    whole = (whole * factor).astype(jnp.bfloat16).reshape(tokens, heads, 2, width)
    grad_keys = whole[:, :, 0].reshape(1, tokens, heads * width)
    grad_values = whole[:, :, 1].reshape(1, tokens, heads * width)
    return (attended[None], grad_queries[None], grad_keys, grad_values)


def solution(mesh):
    placed = (
        P("dp", "ctx", None),
        P("dp", "ctx", None),
        P("dp", "ctx", None),
        P("dp", "ctx", None),
        P("dp", None),
        P("dp", None),
        P("dp", "ctx"),
    )
    return jax.shard_map(
        shards,
        mesh=mesh,
        in_specs=placed,
        out_specs=(
            P("dp", "ctx", None),
            P("dp", "ctx", None),
            P("dp", "ctx", None),
            P("dp", "ctx", None),
        ),
        check_vma=False,
    )
```

```python
import math

import jax
import jax.numpy as jnp
from jax import lax
from jax.experimental import pallas as pl
from jax.experimental.pallas import tpu as pltpu
from jax.sharding import PartitionSpec as P

HEAD_WIDTH = 128
QUERY_HEADS = 32
KEY_VALUE_HEADS = 4
ALIGN_TOKENS = 64
MOST = 8
GROUP = QUERY_HEADS // KEY_VALUE_HEADS
SPAN = MOST * ALIGN_TOKENS
LOG2E = math.log2(math.e)
SCALE = 1.0 / math.sqrt(HEAD_WIDTH)
HIDDEN = -1e30


def dot_nt(a, b):
    return lax.dot_general(a, b, (((1,), (1,)), ((), ())), preferred_element_type=jnp.float32)


def dot_nn(a, b):
    return lax.dot_general(a, b, (((1,), (0,)), ((), ())), preferred_element_type=jnp.float32)


def dot_tn(a, b):
    return lax.dot_general(a, b, (((0,), (0,)), ((), ())), preferred_element_type=jnp.float32)


def fold_rows(x, op):
    folded = x[:8]
    for i in range(8, x.shape[0], 8):
        folded = op(folded, x[i : i + 8])
    return folded


def attention_kernel(
    back_ref,
    q_ref,
    g_ref,
    own_ref,
    near_ref,
    mid_ref,
    far_ref,
    fourth_ref,
    out_ref,
    dq_ref,
    own_part,
    near_part,
    mid_part,
    far_part,
    fourth_part,
    keys_acc,
    values_acc,
):
    width, block = HEAD_WIDTH, ALIGN_TOKENS
    shards_in = (fourth_ref, far_ref, mid_ref, near_ref, own_ref)
    keys = jnp.concatenate([ref[0] for ref in shards_in], axis=0)
    values = jnp.concatenate([ref[1] for ref in shards_in], axis=0)
    rows, tokens = keys.shape[0], own_ref.shape[1]
    count, cols = tokens // block, GROUP * block
    causal = lax.broadcasted_iota(jnp.int32, (block, cols), 0) <= (
        lax.broadcasted_iota(jnp.int32, (block, cols), 1) & (block - 1)
    )

    def heads_stacked(ref, t):
        return jnp.concatenate(
            [
                ref[t * block : (t + 1) * block, h * width : (h + 1) * width]
                for h in range(GROUP)
            ],
            axis=0,
        )

    def window(t):
        lo = rows - SPAN - (count - 1 - t) * block
        return slice(lo, lo + SPAN)

    def probabilities(t, s, dp):
        hidden = [jnp.where(b >= MOST - 1 - back_ref[t], 0.0, HIDDEN) for b in range(MOST - 1)]
        hidden.append(0.0)
        s = [s[b * block : (b + 1) * block] for b in range(MOST)]
        s[-1] = jnp.where(causal, s[-1], HIDDEN)
        dp = [dp[b * block : (b + 1) * block] for b in range(MOST)]
        peak = None
        for b in range(MOST):
            part = fold_rows(s[b], jnp.maximum) + hidden[b]
            peak = part if peak is None else jnp.maximum(peak, part)
        peak = jnp.max(peak, axis=0, keepdims=True)
        e, total, weighed = [], None, None
        for b in range(MOST):
            e.append(jnp.exp2((s[b] - (peak - hidden[b])) * (SCALE * LOG2E)))
            part, part_weighed = fold_rows(e[b], jnp.add), fold_rows(e[b] * dp[b], jnp.add)
            total = part if total is None else total + part
            weighed = part_weighed if weighed is None else weighed + part_weighed
        inverse = 1.0 / jnp.sum(total, axis=0, keepdims=True)
        delta = jnp.sum(weighed, axis=0, keepdims=True) * inverse
        p_low, ds = [], []
        for b in range(MOST):
            p = e[b] * inverse
            p_low.append(p.astype(jnp.bfloat16))
            ds.append((p * (dp[b] - delta)).astype(jnp.bfloat16))
        return jnp.concatenate(p_low, axis=0), jnp.concatenate(ds, axis=0)

    keys_acc[...] = jnp.zeros_like(keys_acc)
    values_acc[...] = jnp.zeros_like(values_acc)
    products = [
        (
            dot_nt(keys[window(t)], heads_stacked(q_ref, t)),
            dot_nt(values[window(t)], heads_stacked(g_ref, t)),
        )
        for t in range(count)
    ]
    for t in range(count):
        p_low, ds = probabilities(t, *products[t])
        keys_acc[window(t), :] += dot_nn(ds, heads_stacked(q_ref, t))
        values_acc[window(t), :] += dot_nn(p_low, heads_stacked(g_ref, t))
        out = dot_tn(p_low, values[window(t)]).astype(jnp.bfloat16)
        dq = (dot_tn(ds, keys[window(t)]) * SCALE).astype(jnp.bfloat16)
        for h in range(GROUP):
            place = (slice(t * block, (t + 1) * block), slice(h * width, (h + 1) * width))
            out_ref[place] = out[h * block : (h + 1) * block]
            dq_ref[place] = dq[h * block : (h + 1) * block]
    for i, ref in enumerate((fourth_part, far_part, mid_part, near_part, own_part)):
        part = slice(i * tokens, (i + 1) * tokens)
        ref[0] = (keys_acc[part, :] * SCALE).astype(ref.dtype)
        ref[1] = values_acc[part, :].astype(ref.dtype)


def in_hbm(array):
    return pltpu.with_memory_space_constraint(array, pltpu.HBM)


def attention(back, queries, grads, own, near, mid, far, fourth):
    tokens = queries.shape[0]
    wide = pl.BlockSpec((tokens, GROUP * HEAD_WIDTH), lambda i, *_: (0, i))
    pair = pl.BlockSpec((2, tokens, HEAD_WIDTH), lambda i, *_: (0, 0, i))
    shape = jax.ShapeDtypeStruct
    return pl.pallas_call(
        attention_kernel,
        grid_spec=pltpu.PrefetchScalarGridSpec(
            num_scalar_prefetch=1,
            grid=(KEY_VALUE_HEADS,),
            in_specs=[wide] * 2 + [pair] * 5,
            out_specs=[wide] * 2 + [pair] * 5,
            scratch_shapes=[pltpu.VMEM((5 * tokens, HEAD_WIDTH), jnp.float32)] * 2,
        ),
        out_shape=[shape(queries.shape, jnp.bfloat16)] * 2
        + [pltpu.HBM(own.shape, jnp.float32)]
        + [shape(own.shape, jnp.bfloat16)] * 4,
        compiler_params=pltpu.CompilerParams(vmem_limit_bytes=48 * 1024 * 1024),
        name="attention",
    )(back, queries, grads, own, *(in_hbm(x) for x in (near, mid, far, fourth)))


def blocks_back(lengths, order, first, count):
    ends = jnp.sum(
        jnp.where(
            jnp.arange(lengths.shape[0])[:, None] >= jnp.arange(lengths.shape[0])[None, :],
            lengths[None, :],
            0,
        ),
        axis=1,
    )
    places = lax.dynamic_slice_in_dim(order, first, count, 0)
    starts = jnp.max(jnp.where(ends[None, :] <= places[:, None], ends[None, :], 0), axis=1)
    return places - starts


def axis_total(value, axis):
    n = lax.axis_size(axis)
    sent = jnp.broadcast_to(value, (n, 1, HEAD_WIDTH))
    return jnp.sum(lax.all_to_all(sent, axis, split_axis=0, concat_axis=0)[:, 0, 0])


def after(value, *others):
    return lax.optimization_barrier((value, *others))[0]


def shards(
    queries, key_head_states, value_head_states, out_grad, doc_blocks, block_order, target_mask
):
    tokens = queries.shape[1]
    ctx_count = lax.axis_size("ctx")
    pack_rows = tokens * ctx_count

    def shift(array, steps):
        pairs = [(i, (i + steps) % ctx_count) for i in range(ctx_count)]
        return lax.ppermute(array, "ctx", pairs)

    own = jnp.concatenate([key_head_states, value_head_states], axis=0)
    fourth = shift(own, 4)
    near = shift(own, 1)
    pack_total = axis_total(jnp.sum(target_mask.astype(jnp.float32)), "ctx")
    mid = shift(near, 1)
    far = shift(fourth, -1)
    grads = out_grad[0] * target_mask[0].astype(jnp.bfloat16)[:, None]
    blocks = tokens // ALIGN_TOKENS
    back = blocks_back(doc_blocks[0], block_order[0], lax.axis_index("ctx") * blocks, blocks)
    back = after(back, pack_total)
    attended, dq, own_part, near_part, mid_part, far_part, fourth_part = attention(
        back, queries[0], grads, own, near, mid, far, fourth
    )
    mid_back = shift(mid_part, -1)
    far_on = shift(far_part, 1)
    near_sum = near_part + mid_back
    fourth_sum = fourth_part + far_on
    fourth_back = shift(fourth_sum, -4)
    near_back = shift(near_sum, -1)
    whole = own_part + near_back.astype(jnp.float32) + fourth_back.astype(jnp.float32)
    total = axis_total(after(pack_total, near_sum, fourth_sum), "dp")
    factor = lax.axis_size("dp") * pack_rows / after(total, whole)
    grad_queries = (dq.astype(jnp.float32) * factor).astype(jnp.bfloat16)
    whole = (whole * factor).astype(jnp.bfloat16)
    return (attended[None], grad_queries[None], whole[:1], whole[1:])


def solution(mesh):
    placed = (
        P("dp", "ctx", None),
        P("dp", "ctx", None),
        P("dp", "ctx", None),
        P("dp", "ctx", None),
        P("dp", None),
        P("dp", None),
        P("dp", "ctx"),
    )
    return jax.shard_map(
        shards,
        mesh=mesh,
        in_specs=placed,
        out_specs=(
            P("dp", "ctx", None),
            P("dp", "ctx", None),
            P("dp", "ctx", None),
            P("dp", "ctx", None),
        ),
        check_vma=False,
    )
```

```python
import math

import jax
import jax.numpy as jnp
from jax import lax
from jax.experimental import pallas as pl
from jax.experimental.pallas import tpu as pltpu
from jax.sharding import PartitionSpec as P

HEAD_WIDTH = 128
QUERY_HEADS = 32
KEY_VALUE_HEADS = 4
ALIGN_TOKENS = 64
MOST = 8
PACK_TOKENS = 4096
GROUP = QUERY_HEADS // KEY_VALUE_HEADS
SPAN = MOST * ALIGN_TOKENS
LOG2E = math.log2(math.e)
SCALE = 1.0 / math.sqrt(HEAD_WIDTH)
HIDDEN = -1e30
QUERY_PIECES = 4


def dot_nt(a, b):
    return lax.dot_general(a, b, (((1,), (1,)), ((), ())), preferred_element_type=jnp.float32)


def dot_nn(a, b):
    return lax.dot_general(a, b, (((1,), (0,)), ((), ())), preferred_element_type=jnp.float32)


def dot_tn(a, b):
    return lax.dot_general(a, b, (((0,), (0,)), ((), ())), preferred_element_type=jnp.float32)


def fold_rows(x, op):
    folded = x[:8]
    for i in range(8, x.shape[0], 8):
        folded = op(folded, x[i : i + 8])
    return folded


def attention_kernel(
    back_ref,
    q_ref,
    g_ref,
    own_ref,
    near_ref,
    mid_ref,
    far_ref,
    fourth_ref,
    out_ref,
    dq_ref,
    own_part,
    near_part,
    mid_part,
    far_part,
    fourth_part,
    keys_acc,
    values_acc,
):
    width, block = HEAD_WIDTH, ALIGN_TOKENS
    group = GROUP * width
    shards_in = (fourth_ref, far_ref, mid_ref, near_ref, own_ref)
    tokens = own_ref.shape[1]
    rows, count, cols = len(shards_in) * tokens, tokens // block, GROUP * block
    causal = lax.broadcasted_iota(jnp.int32, (block, cols), 0) <= (
        lax.broadcasted_iota(jnp.int32, (block, cols), 1) & (block - 1)
    )

    def stacked(ref, k, t):
        at, first = slice(t * block, (t + 1) * block), k * GROUP
        return [
            ref[at, h * width : (h + 1) * width] for h in range(first, first + GROUP)
        ]

    def query_rows(k, t):
        return jnp.concatenate(stacked(q_ref, k, t), axis=0)

    def grad_rows(k, t):
        return jnp.concatenate(stacked(g_ref, k, t), axis=0)

    def halo(k, side):
        at = slice(k * width, (k + 1) * width)
        return jnp.concatenate([ref[side, :, at] for ref in shards_in], axis=0)

    def window(t):
        lo = rows - SPAN - (count - 1 - t) * block
        return slice(lo, lo + SPAN)

    def probabilities(t, s, dp):
        hidden = [jnp.where(b >= MOST - 1 - back_ref[t], 0.0, HIDDEN) for b in range(MOST - 1)]
        hidden.append(0.0)
        s = [s[b * block : (b + 1) * block] for b in range(MOST)]
        s[-1] = jnp.where(causal, s[-1], HIDDEN)
        dp = [dp[b * block : (b + 1) * block] for b in range(MOST)]
        peak = None
        for b in range(MOST):
            part = fold_rows(s[b], jnp.maximum) + hidden[b]
            peak = part if peak is None else jnp.maximum(peak, part)
        peak = jnp.max(peak, axis=0, keepdims=True)
        e, total, weighed = [], None, None
        for b in range(MOST):
            e.append(jnp.exp2((s[b] - (peak - hidden[b])) * (SCALE * LOG2E)))
            part, part_weighed = fold_rows(e[b], jnp.add), fold_rows(e[b] * dp[b], jnp.add)
            total = part if total is None else total + part
            weighed = part_weighed if weighed is None else weighed + part_weighed
        inverse = 1.0 / jnp.sum(total, axis=0, keepdims=True)
        delta = jnp.sum(weighed, axis=0, keepdims=True) * inverse
        p_low, ds = [], []
        for b in range(MOST):
            p = e[b] * inverse
            p_low.append(p.astype(jnp.bfloat16))
            ds.append((p * (dp[b] - delta)).astype(jnp.bfloat16))
        return jnp.concatenate(p_low, axis=0), jnp.concatenate(ds, axis=0)

    def products(k, t, keys, values):
        return (
            dot_nt(keys[window(t)], query_rows(k, t)),
            dot_nt(values[window(t)], grad_rows(k, t)),
        )

    steps = [(k, t) for k in range(KEY_VALUE_HEADS) for t in range(count)]
    sides = {k: (halo(k, 0), halo(k, 1)) for k in range(KEY_VALUE_HEADS)}
    ahead = products(*steps[0], *sides[0])
    for n, (k, t) in enumerate(steps):
        now = ahead
        if n + 1 < len(steps):
            ahead = products(*steps[n + 1], *sides[steps[n + 1][0]])
        if t == 0:
            keys_acc[...] = jnp.zeros_like(keys_acc)
            values_acc[...] = jnp.zeros_like(values_acc)
        keys, values = sides[k]
        p_low, ds = probabilities(t, *now)
        keys_acc[window(t), :] += dot_nn(ds, query_rows(k, t))
        values_acc[window(t), :] += dot_nn(p_low, grad_rows(k, t))
        out = dot_tn(p_low, values[window(t)]).astype(jnp.bfloat16)
        dq = (dot_tn(ds, keys[window(t)]) * SCALE).astype(jnp.bfloat16)
        place = (slice(t * block, (t + 1) * block), slice(k * group, (k + 1) * group))
        for ref, heads in ((out_ref, out), (dq_ref, dq)):
            ref[place] = jnp.concatenate(
                [heads[h * block : (h + 1) * block] for h in range(GROUP)], axis=1
            )
        if t == count - 1:
            at = slice(k * width, (k + 1) * width)
            for i, ref in enumerate((fourth_part, far_part, mid_part, near_part, own_part)):
                part = slice(i * tokens, (i + 1) * tokens)
                ref[0, :, at] = (keys_acc[part, :] * SCALE).astype(ref.dtype)
                ref[1, :, at] = values_acc[part, :].astype(ref.dtype)


def attention(back, queries, grads, halo):
    tokens = queries.shape[0]
    whole = pl.BlockSpec(memory_space=pltpu.VMEM)
    shape = jax.ShapeDtypeStruct
    return pl.pallas_call(
        attention_kernel,
        in_specs=[pl.BlockSpec(memory_space=pltpu.SMEM)] + [whole] * 7,
        out_specs=[whole] * 7,
        scratch_shapes=[pltpu.VMEM((5 * tokens, HEAD_WIDTH), jnp.float32)] * 2,
        out_shape=[shape(queries.shape, jnp.bfloat16)] * 2
        + [shape(halo[0].shape, jnp.float32)]
        + [shape(halo[0].shape, jnp.bfloat16)] * 4,
        compiler_params=pltpu.CompilerParams(vmem_limit_bytes=40 * 1024 * 1024),
        name="attention",
    )(back, queries, grads, *halo)


def total_kernel(rows_ref, out_ref):
    rows = rows_ref[...].astype(jnp.float32)
    first = lax.broadcasted_iota(jnp.int32, rows.shape, rows.ndim - 1) == 0
    if rows.shape[0] > 1:
        rows = jnp.where(first, rows, 0.0)
    out_ref[...] = jnp.full(out_ref.shape, jnp.sum(rows), jnp.float32)


def kept_kernel(mask_ref, grads_ref, kept_ref):
    tokens, width = mask_ref.shape[1], HEAD_WIDTH
    mask = jnp.broadcast_to(mask_ref[...].astype(jnp.float32), (width, tokens))
    mask = jnp.transpose(mask).astype(jnp.bfloat16)
    for h in range(grads_ref.shape[1] // width):
        at = slice(h * width, (h + 1) * width)
        kept_ref[:, at] = grads_ref[:, at] * mask


def kept_grads(mask, grads):
    columns = pl.BlockSpec((grads.shape[0], GROUP * HEAD_WIDTH), lambda i: (0, i))
    return pl.pallas_call(
        kept_kernel,
        grid=(KEY_VALUE_HEADS,),
        in_specs=[pl.BlockSpec(mask.shape, lambda i: (0, 0)), columns],
        out_specs=columns,
        out_shape=jax.ShapeDtypeStruct(grads.shape, grads.dtype),
        cost_estimate=pl.CostEstimate(flops=0, bytes_accessed=0, transcendentals=0),
        name="kept_grads",
    )(mask, grads)


def spread_total(rows, copies, space=None):
    return pl.pallas_call(
        total_kernel,
        in_specs=[pl.BlockSpec(memory_space=space)],
        out_shape=jax.ShapeDtypeStruct((copies, 1, HEAD_WIDTH), jnp.float32),
        name="spread_total",
    )(rows)


def gradients_kernel(
    rows_ref,
    dq_ref,
    own_ref,
    near_ref,
    fourth_ref,
    grad_queries_ref,
    grad_keys_ref,
    grad_values_ref,
    queries_out,
    sides_out,
    sems,
):
    tokens_in_all = rows_ref.shape[0] * PACK_TOKENS
    first = lax.broadcasted_iota(jnp.int32, rows_ref.shape, 2) == 0
    factor = tokens_in_all / jnp.sum(jnp.where(first, rows_ref[...], 0.0))
    copies = []
    rows = dq_ref.shape[0] // QUERY_PIECES
    for i in range(QUERY_PIECES):
        at = slice(i * rows, (i + 1) * rows)
        queries_out[at] = (dq_ref[at].astype(jnp.float32) * factor).astype(jnp.bfloat16)
        copies.append(
            pltpu.make_async_copy(queries_out.at[at], grad_queries_ref.at[at], sems.at[i])
        )
        copies[-1].start()
    for side, ref in enumerate((grad_keys_ref, grad_values_ref)):
        back = near_ref[side].astype(jnp.float32) + fourth_ref[side].astype(jnp.float32)
        sides_out[side] = ((own_ref[side] + back) * factor).astype(jnp.bfloat16)
        copies.append(
            pltpu.make_async_copy(sides_out.at[side], ref, sems.at[QUERY_PIECES + side])
        )
        copies[-1].start()
    for copy in copies:
        copy.wait()


def gradients(rows, dq, own_part, near_back, fourth_back):
    narrow = jax.ShapeDtypeStruct(own_part.shape[1:], jnp.bfloat16)
    return pl.pallas_call(
        gradients_kernel,
        in_specs=[pl.BlockSpec(memory_space=pltpu.VMEM)] * 5,
        out_specs=[pl.BlockSpec(memory_space=pltpu.HBM)] * 3,
        out_shape=[jax.ShapeDtypeStruct(dq.shape, jnp.bfloat16), narrow, narrow],
        scratch_shapes=[
            pltpu.VMEM(dq.shape, jnp.bfloat16),
            pltpu.VMEM(own_part.shape, jnp.bfloat16),
            pltpu.SemaphoreType.DMA((QUERY_PIECES + 2,)),
        ],
        compiler_params=pltpu.CompilerParams(vmem_limit_bytes=24 * 1024 * 1024),
        name="gradients",
    )(rows, dq, own_part, near_back, fourth_back)


def exchanged(rows, axis):
    return lax.all_to_all(rows, axis, split_axis=0, concat_axis=0)


def blocks_back(lengths, order, first, count):
    ends = jnp.sum(
        jnp.where(
            jnp.arange(lengths.shape[0])[:, None] >= jnp.arange(lengths.shape[0])[None, :],
            lengths[None, :],
            0,
        ),
        axis=1,
    )
    places = lax.dynamic_slice_in_dim(order, first, count, 0)
    starts = jnp.max(jnp.where(ends[None, :] <= places[:, None], ends[None, :], 0), axis=1)
    return places - starts


def after(value, *others):
    return lax.optimization_barrier((value, *others))[0]


def shards(
    queries, key_head_states, value_head_states, out_grad, doc_blocks, block_order, target_mask
):
    tokens = queries.shape[1]
    ctx_count = lax.axis_size("ctx")

    def shift(array, steps):
        pairs = [(i, (i + steps) % ctx_count) for i in range(ctx_count)]
        return lax.ppermute(array, "ctx", pairs)

    side = lax.broadcasted_iota(jnp.int32, (2, 1, 1), 0)
    own = jnp.where(side == 0, key_head_states, value_head_states)
    fourth = shift(own, 4)
    near = shift(own, 1)
    counts = exchanged(spread_total(target_mask, ctx_count), "ctx")
    mid = shift(near, 1)
    far = shift(fourth, -1)
    pack_counts = spread_total(counts, lax.axis_size("dp"), pltpu.VMEM)
    blocks = tokens // ALIGN_TOKENS
    back = blocks_back(doc_blocks[0], block_order[0], lax.axis_index("ctx") * blocks, blocks)
    back = after(back, pack_counts)
    grads = kept_grads(after(target_mask, near, fourth), out_grad[0])
    attended, dq, own_part, near_part, mid_part, far_part, fourth_part = attention(
        back, queries[0], grads, (own, near, mid, far, fourth)
    )
    mid_back = shift(mid_part, -1)
    far_on = shift(far_part, 1)
    near_sum = near_part + mid_back
    fourth_sum = fourth_part + far_on
    fourth_back = shift(fourth_sum, -4)
    near_back = shift(near_sum, -1)
    counts = exchanged(after(pack_counts, near_sum, fourth_sum), "dp")
    grad_queries, grad_keys, grad_values = gradients(counts, dq, own_part, near_back, fourth_back)
    return (attended[None], grad_queries[None], grad_keys[None], grad_values[None])


def solution(mesh):
    placed = (
        P("dp", "ctx", None),
        P("dp", "ctx", None),
        P("dp", "ctx", None),
        P("dp", "ctx", None),
        P("dp", None),
        P("dp", None),
        P("dp", "ctx"),
    )
    return jax.shard_map(
        shards,
        mesh=mesh,
        in_specs=placed,
        out_specs=(
            P("dp", "ctx", None),
            P("dp", "ctx", None),
            P("dp", "ctx", None),
            P("dp", "ctx", None),
        ),
        check_vma=False,
    )
```

```python
import math

import jax
import jax.numpy as jnp
from jax import lax
from jax.experimental import pallas as pl
from jax.experimental.pallas import tpu as pltpu
from jax.sharding import PartitionSpec as P

HEAD_WIDTH = 128
QUERY_HEADS = 32
KEY_VALUE_HEADS = 4
ALIGN_TOKENS = 64
MOST = 8
PACK_TOKENS = 4096
GROUP = QUERY_HEADS // KEY_VALUE_HEADS
SPAN = MOST * ALIGN_TOKENS
LOG2E = math.log2(math.e)
SCALE = 1.0 / math.sqrt(HEAD_WIDTH)
HIDDEN = -1e30
QUERY_PIECES = 4


def dot_nt(a, b):
    return lax.dot_general(a, b, (((1,), (1,)), ((), ())), preferred_element_type=jnp.float32)


def dot_nn(a, b):
    return lax.dot_general(a, b, (((1,), (0,)), ((), ())), preferred_element_type=jnp.float32)


def dot_tn(a, b):
    return lax.dot_general(a, b, (((0,), (0,)), ((), ())), preferred_element_type=jnp.float32)


def fold_rows(x, op):
    folded = x[:8]
    for i in range(8, x.shape[0], 8):
        folded = op(folded, x[i : i + 8])
    return folded


def attention_kernel(
    back_ref,
    q_ref,
    g_ref,
    own_ref,
    near_ref,
    mid_ref,
    far_ref,
    fourth_ref,
    out_ref,
    dq_ref,
    own_part,
    near_part,
    mid_part,
    far_part,
    fourth_part,
    keys_acc,
    values_acc,
):
    width, block = HEAD_WIDTH, ALIGN_TOKENS
    group = GROUP * width
    shards_in = (fourth_ref, far_ref, mid_ref, near_ref, own_ref)
    tokens = own_ref.shape[1]
    rows, count, cols = len(shards_in) * tokens, tokens // block, GROUP * block
    causal = lax.broadcasted_iota(jnp.int32, (block, cols), 0) <= (
        lax.broadcasted_iota(jnp.int32, (block, cols), 1) & (block - 1)
    )

    def stacked(ref, k, t):
        at, first = slice(t * block, (t + 1) * block), k * GROUP
        return [
            ref[at, h * width : (h + 1) * width] for h in range(first, first + GROUP)
        ]

    def query_rows(k, t):
        return jnp.concatenate(stacked(q_ref, k, t), axis=0)

    def grad_rows(k, t):
        return jnp.concatenate(stacked(g_ref, k, t), axis=0)

    def halo(k, side):
        at = slice(k * width, (k + 1) * width)
        return jnp.concatenate([ref[side, :, at] for ref in shards_in], axis=0)

    def window(t):
        lo = rows - SPAN - (count - 1 - t) * block
        return slice(lo, lo + SPAN)

    def probabilities(t, s, dp):
        hidden = [jnp.where(b >= MOST - 1 - back_ref[t], 0.0, HIDDEN) for b in range(MOST - 1)]
        hidden.append(0.0)
        s = [s[b * block : (b + 1) * block] for b in range(MOST)]
        s[-1] = jnp.where(causal, s[-1], HIDDEN)
        dp = [dp[b * block : (b + 1) * block] for b in range(MOST)]
        peak = None
        for b in range(MOST):
            part = fold_rows(s[b], jnp.maximum) + hidden[b]
            peak = part if peak is None else jnp.maximum(peak, part)
        peak = jnp.max(peak, axis=0, keepdims=True)
        e, total, weighed = [], None, None
        for b in range(MOST):
            e.append(jnp.exp2((s[b] - (peak - hidden[b])) * (SCALE * LOG2E)))
            part, part_weighed = fold_rows(e[b], jnp.add), fold_rows(e[b] * dp[b], jnp.add)
            total = part if total is None else total + part
            weighed = part_weighed if weighed is None else weighed + part_weighed
        inverse = 1.0 / jnp.sum(total, axis=0, keepdims=True)
        delta = jnp.sum(weighed, axis=0, keepdims=True) * inverse
        p_low, ds = [], []
        for b in range(MOST):
            p = e[b] * inverse
            p_low.append(p.astype(jnp.bfloat16))
            ds.append((p * (dp[b] - delta)).astype(jnp.bfloat16))
        return jnp.concatenate(p_low, axis=0), jnp.concatenate(ds, axis=0)

    def products(k, t, keys, values):
        return (
            dot_nt(keys[window(t)], query_rows(k, t)),
            dot_nt(values[window(t)], grad_rows(k, t)),
        )

    steps = [(k, t) for k in range(KEY_VALUE_HEADS) for t in range(count)]
    sides = {k: (halo(k, 0), halo(k, 1)) for k in range(KEY_VALUE_HEADS)}
    ahead = products(*steps[0], *sides[0])
    for n, (k, t) in enumerate(steps):
        now = ahead
        if n + 1 < len(steps):
            ahead = products(*steps[n + 1], *sides[steps[n + 1][0]])
        if t == 0:
            keys_acc[...] = jnp.zeros_like(keys_acc)
            values_acc[...] = jnp.zeros_like(values_acc)
        keys, values = sides[k]
        p_low, ds = probabilities(t, *now)
        keys_acc[window(t), :] += dot_nn(ds, query_rows(k, t))
        values_acc[window(t), :] += dot_nn(p_low, grad_rows(k, t))
        out = dot_tn(p_low, values[window(t)]).astype(jnp.bfloat16)
        dq = (dot_tn(ds, keys[window(t)]) * SCALE).astype(jnp.bfloat16)
        place = (slice(t * block, (t + 1) * block), slice(k * group, (k + 1) * group))
        for ref, heads in ((out_ref, out), (dq_ref, dq)):
            ref[place] = jnp.concatenate(
                [heads[h * block : (h + 1) * block] for h in range(GROUP)], axis=1
            )
        if t == count - 1:
            at = slice(k * width, (k + 1) * width)
            for i, ref in enumerate((fourth_part, far_part, mid_part, near_part, own_part)):
                part = slice(i * tokens, (i + 1) * tokens)
                ref[0, :, at] = (keys_acc[part, :] * SCALE).astype(ref.dtype)
                ref[1, :, at] = values_acc[part, :].astype(ref.dtype)


def attention(back, queries, grads, halo):
    tokens = queries.shape[0]
    whole = pl.BlockSpec(memory_space=pltpu.VMEM)
    shape = jax.ShapeDtypeStruct
    return pl.pallas_call(
        attention_kernel,
        in_specs=[pl.BlockSpec(memory_space=pltpu.SMEM)] + [whole] * 7,
        out_specs=[whole] * 7,
        scratch_shapes=[pltpu.VMEM((5 * tokens, HEAD_WIDTH), jnp.float32)] * 2,
        out_shape=[shape(queries.shape, jnp.bfloat16)] * 2
        + [shape(halo[0].shape, jnp.float32)]
        + [shape(halo[0].shape, jnp.bfloat16)] * 4,
        compiler_params=pltpu.CompilerParams(vmem_limit_bytes=40 * 1024 * 1024),
        name="attention",
    )(back, queries, grads, *halo)


def total_kernel(rows_ref, out_ref):
    rows = rows_ref[...].astype(jnp.float32)
    first = lax.broadcasted_iota(jnp.int32, rows.shape, rows.ndim - 1) == 0
    if rows.shape[0] > 1:
        rows = jnp.where(first, rows, 0.0)
    out_ref[...] = jnp.full(out_ref.shape, jnp.sum(rows), jnp.float32)


def kept_kernel(mask_ref, grads_ref, kept_ref):
    tokens, width = mask_ref.shape[1], HEAD_WIDTH
    mask = jnp.broadcast_to(mask_ref[...].astype(jnp.float32), (width, tokens))
    mask = jnp.transpose(mask).astype(jnp.bfloat16)
    for h in range(grads_ref.shape[1] // width):
        at = slice(h * width, (h + 1) * width)
        kept_ref[:, at] = grads_ref[:, at] * mask


def kept_grads(mask, grads):
    return pl.pallas_call(
        kept_kernel,
        out_specs=pl.BlockSpec(memory_space=pltpu.VMEM),
        out_shape=pltpu.VMEM(grads.shape, grads.dtype),
        cost_estimate=pl.CostEstimate(flops=0, bytes_accessed=0, transcendentals=0),
        name="kept_grads",
    )(mask, grads)


def spread_total(rows, copies, space=None):
    return pl.pallas_call(
        total_kernel,
        in_specs=[pl.BlockSpec(memory_space=space)],
        out_shape=jax.ShapeDtypeStruct((copies, 1, HEAD_WIDTH), jnp.float32),
        name="spread_total",
    )(rows)


def gradients_kernel(
    rows_ref,
    dq_ref,
    own_ref,
    near_ref,
    fourth_ref,
    grad_queries_ref,
    grad_keys_ref,
    grad_values_ref,
    queries_out,
    sides_out,
    sems,
):
    tokens_in_all = rows_ref.shape[0] * PACK_TOKENS
    first = lax.broadcasted_iota(jnp.int32, rows_ref.shape, 2) == 0
    factor = tokens_in_all / jnp.sum(jnp.where(first, rows_ref[...], 0.0))
    copies = []
    rows = dq_ref.shape[0] // QUERY_PIECES
    for i in range(QUERY_PIECES):
        at = slice(i * rows, (i + 1) * rows)
        queries_out[at] = (dq_ref[at].astype(jnp.float32) * factor).astype(jnp.bfloat16)
        copies.append(
            pltpu.make_async_copy(queries_out.at[at], grad_queries_ref.at[at], sems.at[i])
        )
        copies[-1].start()
    for side, ref in enumerate((grad_keys_ref, grad_values_ref)):
        back = near_ref[side].astype(jnp.float32) + fourth_ref[side].astype(jnp.float32)
        sides_out[side] = ((own_ref[side] + back) * factor).astype(jnp.bfloat16)
        copies.append(
            pltpu.make_async_copy(sides_out.at[side], ref, sems.at[QUERY_PIECES + side])
        )
        copies[-1].start()
    for copy in copies:
        copy.wait()


def gradients(rows, dq, own_part, near_back, fourth_back):
    narrow = jax.ShapeDtypeStruct(own_part.shape[1:], jnp.bfloat16)
    return pl.pallas_call(
        gradients_kernel,
        in_specs=[pl.BlockSpec(memory_space=pltpu.VMEM)] * 5,
        out_specs=[pl.BlockSpec(memory_space=pltpu.HBM)] * 3,
        out_shape=[jax.ShapeDtypeStruct(dq.shape, jnp.bfloat16), narrow, narrow],
        scratch_shapes=[
            pltpu.VMEM(dq.shape, jnp.bfloat16),
            pltpu.VMEM(own_part.shape, jnp.bfloat16),
            pltpu.SemaphoreType.DMA((QUERY_PIECES + 2,)),
        ],
        compiler_params=pltpu.CompilerParams(vmem_limit_bytes=24 * 1024 * 1024),
        name="gradients",
    )(rows, dq, own_part, near_back, fourth_back)


def exchanged(rows, axis):
    return lax.all_to_all(rows, axis, split_axis=0, concat_axis=0)


def blocks_back(lengths, order, first, count):
    ends = jnp.sum(
        jnp.where(
            jnp.arange(lengths.shape[0])[:, None] >= jnp.arange(lengths.shape[0])[None, :],
            lengths[None, :],
            0,
        ),
        axis=1,
    )
    places = lax.dynamic_slice_in_dim(order, first, count, 0)
    starts = jnp.max(jnp.where(ends[None, :] <= places[:, None], ends[None, :], 0), axis=1)
    return places - starts


def after(value, *others):
    return lax.optimization_barrier((value, *others))[0]


def shards(
    queries, key_head_states, value_head_states, out_grad, doc_blocks, block_order, target_mask
):
    tokens = queries.shape[1]
    ctx_count = lax.axis_size("ctx")

    def shift(array, steps):
        pairs = [(i, (i + steps) % ctx_count) for i in range(ctx_count)]
        return lax.ppermute(array, "ctx", pairs)

    side = lax.broadcasted_iota(jnp.int32, (2, 1, 1), 0)
    own = jnp.where(side == 0, key_head_states, value_head_states)
    fourth = shift(own, 4)
    near = shift(own, 1)
    counts = exchanged(spread_total(target_mask, ctx_count), "ctx")
    mid = shift(near, 1)
    far = shift(fourth, -1)
    pack_counts = spread_total(counts, lax.axis_size("dp"), pltpu.VMEM)
    blocks = tokens // ALIGN_TOKENS
    back = blocks_back(doc_blocks[0], block_order[0], lax.axis_index("ctx") * blocks, blocks)
    back = after(back, pack_counts)
    grads = kept_grads(after(target_mask, near, fourth), out_grad[0])
    attended, dq, own_part, near_part, mid_part, far_part, fourth_part = attention(
        back, queries[0], grads, (own, near, mid, far, fourth)
    )
    mid_back = shift(mid_part, -1)
    far_on = shift(far_part, 1)
    near_sum = near_part + mid_back
    fourth_sum = fourth_part + far_on
    fourth_back = shift(fourth_sum, -4)
    near_back = shift(near_sum, -1)
    counts = exchanged(after(pack_counts, near_sum, fourth_sum), "dp")
    grad_queries, grad_keys, grad_values = gradients(counts, dq, own_part, near_back, fourth_back)
    return (attended[None], grad_queries[None], grad_keys[None], grad_values[None])


def solution(mesh):
    placed = (
        P("dp", "ctx", None),
        P("dp", "ctx", None),
        P("dp", "ctx", None),
        P("dp", "ctx", None),
        P("dp", None),
        P("dp", None),
        P("dp", "ctx"),
    )
    return jax.shard_map(
        shards,
        mesh=mesh,
        in_specs=placed,
        out_specs=(
            P("dp", "ctx", None),
            P("dp", "ctx", None),
            P("dp", "ctx", None),
            P("dp", "ctx", None),
        ),
        check_vma=False,
    )
```

```python
import math

import jax
import jax.numpy as jnp
from jax import lax
from jax.experimental import pallas as pl
from jax.experimental.pallas import tpu as pltpu
from jax.sharding import PartitionSpec as P

HEAD_WIDTH = 128
QUERY_HEADS = 32
KEY_VALUE_HEADS = 4
ALIGN_TOKENS = 64
MOST = 8
PACK_TOKENS = 4096
GROUP = QUERY_HEADS // KEY_VALUE_HEADS
SPAN = MOST * ALIGN_TOKENS
LOG2E = math.log2(math.e)
SCALE = 1.0 / math.sqrt(HEAD_WIDTH)
HIDDEN = -1e30
QUERY_PIECES = 4


def dot_nt(a, b):
    return lax.dot_general(a, b, (((1,), (1,)), ((), ())), preferred_element_type=jnp.float32)


def dot_nn(a, b):
    return lax.dot_general(a, b, (((1,), (0,)), ((), ())), preferred_element_type=jnp.float32)


def dot_tn(a, b):
    return lax.dot_general(a, b, (((0,), (0,)), ((), ())), preferred_element_type=jnp.float32)


def fold_rows(x, op):
    folded = x[:8]
    for i in range(8, x.shape[0], 8):
        folded = op(folded, x[i : i + 8])
    return folded


def attention_kernel(
    back_ref,
    q_ref,
    g_ref,
    own_ref,
    near_ref,
    mid_ref,
    far_ref,
    fourth_ref,
    out_ref,
    dq_ref,
    own_part,
    near_part,
    mid_part,
    far_part,
    fourth_part,
    keys_acc,
    values_acc,
):
    width, block = HEAD_WIDTH, ALIGN_TOKENS
    group = GROUP * width
    shards_in = (fourth_ref, far_ref, mid_ref, near_ref, own_ref)
    tokens = own_ref.shape[1]
    rows, count, cols = len(shards_in) * tokens, tokens // block, GROUP * block
    causal = lax.broadcasted_iota(jnp.int32, (block, cols), 0) <= (
        lax.broadcasted_iota(jnp.int32, (block, cols), 1) & (block - 1)
    )

    def stacked(ref, k, t):
        at, first = slice(t * block, (t + 1) * block), k * GROUP
        return [
            ref[at, h * width : (h + 1) * width] for h in range(first, first + GROUP)
        ]

    def query_rows(k, t):
        return jnp.concatenate(stacked(q_ref, k, t), axis=0)

    def grad_rows(k, t):
        return jnp.concatenate(stacked(g_ref, k, t), axis=0)

    def halo(k, side):
        at = slice(k * width, (k + 1) * width)
        return jnp.concatenate([ref[side, :, at] for ref in shards_in], axis=0)

    def window(t):
        lo = rows - SPAN - (count - 1 - t) * block
        return slice(lo, lo + SPAN)

    def probabilities(t, s, dp):
        hidden = [jnp.where(b >= MOST - 1 - back_ref[t], 0.0, HIDDEN) for b in range(MOST - 1)]
        hidden.append(0.0)
        s = [s[b * block : (b + 1) * block] for b in range(MOST)]
        s[-1] = jnp.where(causal, s[-1], HIDDEN)
        dp = [dp[b * block : (b + 1) * block] for b in range(MOST)]
        peak = None
        for b in range(MOST):
            part = fold_rows(s[b], jnp.maximum) + hidden[b]
            peak = part if peak is None else jnp.maximum(peak, part)
        peak = jnp.max(peak, axis=0, keepdims=True)
        e, total, weighed = [], None, None
        for b in range(MOST):
            e.append(jnp.exp2((s[b] - (peak - hidden[b])) * (SCALE * LOG2E)))
            part, part_weighed = fold_rows(e[b], jnp.add), fold_rows(e[b] * dp[b], jnp.add)
            total = part if total is None else total + part
            weighed = part_weighed if weighed is None else weighed + part_weighed
        inverse = 1.0 / jnp.sum(total, axis=0, keepdims=True)
        delta = jnp.sum(weighed, axis=0, keepdims=True) * inverse
        p_low, ds = [], []
        for b in range(MOST):
            p = e[b] * inverse
            p_low.append(p.astype(jnp.bfloat16))
            ds.append((p * (dp[b] - delta)).astype(jnp.bfloat16))
        return jnp.concatenate(p_low, axis=0), jnp.concatenate(ds, axis=0)

    def products(k, t, keys, values):
        return (
            dot_nt(keys[window(t)], query_rows(k, t)),
            dot_nt(values[window(t)], grad_rows(k, t)),
        )

    steps = [(k, t) for k in range(KEY_VALUE_HEADS) for t in range(count)]
    sides = {k: (halo(k, 0), halo(k, 1)) for k in range(KEY_VALUE_HEADS)}
    ahead = products(*steps[0], *sides[0])
    for n, (k, t) in enumerate(steps):
        now = ahead
        if n + 1 < len(steps):
            ahead = products(*steps[n + 1], *sides[steps[n + 1][0]])
        keys, values = sides[k]
        p_low, ds = probabilities(t, *now)
        terms = dot_nn(ds, query_rows(k, t)), dot_nn(p_low, grad_rows(k, t))
        for acc, term in zip((keys_acc, values_acc), terms):
            if t == 0:
                for rest in (slice(0, window(0).start), slice(window(0).stop, rows)):
                    acc[rest, :] = jnp.zeros((rest.stop - rest.start, width), jnp.float32)
                acc[window(0), :] = term
            else:
                acc[window(t), :] += term
        out = dot_tn(p_low, values[window(t)]).astype(jnp.bfloat16)
        dq = (dot_tn(ds, keys[window(t)]) * SCALE).astype(jnp.bfloat16)
        place = (slice(t * block, (t + 1) * block), slice(k * group, (k + 1) * group))
        for ref, heads in ((out_ref, out), (dq_ref, dq)):
            ref[place] = jnp.concatenate(
                [heads[h * block : (h + 1) * block] for h in range(GROUP)], axis=1
            )
        if t == count - 1:
            at = slice(k * width, (k + 1) * width)
            for i, ref in enumerate((fourth_part, far_part, mid_part, near_part, own_part)):
                part = slice(i * tokens, (i + 1) * tokens)
                ref[0, :, at] = (keys_acc[part, :] * SCALE).astype(ref.dtype)
                ref[1, :, at] = values_acc[part, :].astype(ref.dtype)


def attention(back, queries, grads, halo):
    tokens = queries.shape[0]
    whole = pl.BlockSpec(memory_space=pltpu.VMEM)
    shape = jax.ShapeDtypeStruct
    return pl.pallas_call(
        attention_kernel,
        in_specs=[pl.BlockSpec(memory_space=pltpu.SMEM)] + [whole] * 7,
        out_specs=[whole] * 7,
        scratch_shapes=[pltpu.VMEM((5 * tokens, HEAD_WIDTH), jnp.float32)] * 2,
        out_shape=[shape(queries.shape, jnp.bfloat16)] * 2
        + [shape(halo[0].shape, jnp.float32)]
        + [shape(halo[0].shape, jnp.bfloat16)] * 4,
        compiler_params=pltpu.CompilerParams(vmem_limit_bytes=40 * 1024 * 1024),
        name="attention",
    )(back, queries, grads, *halo)


def total_kernel(rows_ref, out_ref):
    rows = rows_ref[...].astype(jnp.float32)
    first = lax.broadcasted_iota(jnp.int32, rows.shape, rows.ndim - 1) == 0
    if rows.shape[0] > 1:
        rows = jnp.where(first, rows, 0.0)
    out_ref[...] = jnp.full(out_ref.shape, jnp.sum(rows), jnp.float32)


def kept_kernel(mask_ref, grads_ref, kept_ref):
    tokens, width = mask_ref.shape[1], HEAD_WIDTH
    mask = jnp.broadcast_to(mask_ref[...].astype(jnp.float32), (width, tokens))
    mask = jnp.transpose(mask).astype(jnp.bfloat16)
    for h in range(grads_ref.shape[1] // width):
        at = slice(h * width, (h + 1) * width)
        kept_ref[:, at] = grads_ref[:, at] * mask


def kept_grads(mask, grads):
    return pl.pallas_call(
        kept_kernel,
        out_specs=pl.BlockSpec(memory_space=pltpu.VMEM),
        out_shape=pltpu.VMEM(grads.shape, grads.dtype),
        cost_estimate=pl.CostEstimate(flops=0, bytes_accessed=0, transcendentals=0),
        name="kept_grads",
    )(mask, grads)


def spread_total(rows, copies, space=None):
    return pl.pallas_call(
        total_kernel,
        in_specs=[pl.BlockSpec(memory_space=space)],
        out_shape=jax.ShapeDtypeStruct((copies, 1, HEAD_WIDTH), jnp.float32),
        name="spread_total",
    )(rows)


def gradients_kernel(
    rows_ref,
    dq_ref,
    own_ref,
    near_ref,
    fourth_ref,
    grad_queries_ref,
    grad_keys_ref,
    grad_values_ref,
    queries_out,
    sides_out,
    sems,
):
    tokens_in_all = rows_ref.shape[0] * PACK_TOKENS
    first = lax.broadcasted_iota(jnp.int32, rows_ref.shape, 2) == 0
    factor = tokens_in_all / jnp.sum(jnp.where(first, rows_ref[...], 0.0))
    copies = []
    rows = dq_ref.shape[0] // QUERY_PIECES
    for i in range(QUERY_PIECES):
        at = slice(i * rows, (i + 1) * rows)
        queries_out[at] = (dq_ref[at].astype(jnp.float32) * factor).astype(jnp.bfloat16)
        copies.append(
            pltpu.make_async_copy(queries_out.at[at], grad_queries_ref.at[at], sems.at[i])
        )
        copies[-1].start()
    for side, ref in enumerate((grad_keys_ref, grad_values_ref)):
        back = near_ref[side].astype(jnp.float32) + fourth_ref[side].astype(jnp.float32)
        sides_out[side] = ((own_ref[side] + back) * factor).astype(jnp.bfloat16)
        copies.append(
            pltpu.make_async_copy(sides_out.at[side], ref, sems.at[QUERY_PIECES + side])
        )
        copies[-1].start()
    for copy in copies:
        copy.wait()


def gradients(rows, dq, own_part, near_back, fourth_back):
    narrow = jax.ShapeDtypeStruct(own_part.shape[1:], jnp.bfloat16)
    return pl.pallas_call(
        gradients_kernel,
        in_specs=[pl.BlockSpec(memory_space=pltpu.VMEM)] * 5,
        out_specs=[pl.BlockSpec(memory_space=pltpu.HBM)] * 3,
        out_shape=[jax.ShapeDtypeStruct(dq.shape, jnp.bfloat16), narrow, narrow],
        scratch_shapes=[
            pltpu.VMEM(dq.shape, jnp.bfloat16),
            pltpu.VMEM(own_part.shape, jnp.bfloat16),
            pltpu.SemaphoreType.DMA((QUERY_PIECES + 2,)),
        ],
        compiler_params=pltpu.CompilerParams(vmem_limit_bytes=24 * 1024 * 1024),
        name="gradients",
    )(rows, dq, own_part, near_back, fourth_back)


def exchanged(rows, axis):
    return lax.all_to_all(rows, axis, split_axis=0, concat_axis=0)


def blocks_back(lengths, order, first, count):
    ends = jnp.sum(
        jnp.where(
            jnp.arange(lengths.shape[0])[:, None] >= jnp.arange(lengths.shape[0])[None, :],
            lengths[None, :],
            0,
        ),
        axis=1,
    )
    places = lax.dynamic_slice_in_dim(order, first, count, 0)
    starts = jnp.max(jnp.where(ends[None, :] <= places[:, None], ends[None, :], 0), axis=1)
    return places - starts


def after(value, *others):
    return lax.optimization_barrier((value, *others))[0]


def shards(
    queries, key_head_states, value_head_states, out_grad, doc_blocks, block_order, target_mask
):
    tokens = queries.shape[1]
    ctx_count = lax.axis_size("ctx")

    def shift(array, steps):
        pairs = [(i, (i + steps) % ctx_count) for i in range(ctx_count)]
        return lax.ppermute(array, "ctx", pairs)

    side = lax.broadcasted_iota(jnp.int32, (2, 1, 1), 0)
    own = jnp.where(side == 0, key_head_states, value_head_states)
    fourth = shift(own, 4)
    near = shift(own, 1)
    counts = exchanged(spread_total(target_mask, ctx_count), "ctx")
    mid = shift(near, 1)
    far = shift(fourth, -1)
    pack_counts = spread_total(counts, lax.axis_size("dp"), pltpu.VMEM)
    blocks = tokens // ALIGN_TOKENS
    back = blocks_back(doc_blocks[0], block_order[0], lax.axis_index("ctx") * blocks, blocks)
    back = after(back, pack_counts)
    grads = kept_grads(after(target_mask, near, fourth), out_grad[0])
    attended, dq, own_part, near_part, mid_part, far_part, fourth_part = attention(
        back, queries[0], grads, (own, near, mid, far, fourth)
    )
    mid_back = shift(mid_part, -1)
    far_on = shift(far_part, 1)
    near_sum = near_part + mid_back
    fourth_sum = fourth_part + far_on
    fourth_back = shift(fourth_sum, -4)
    near_back = shift(near_sum, -1)
    counts = exchanged(after(pack_counts, near_sum, fourth_sum), "dp")
    grad_queries, grad_keys, grad_values = gradients(counts, dq, own_part, near_back, fourth_back)
    return (attended[None], grad_queries[None], grad_keys[None], grad_values[None])


def solution(mesh):
    placed = (
        P("dp", "ctx", None),
        P("dp", "ctx", None),
        P("dp", "ctx", None),
        P("dp", "ctx", None),
        P("dp", None),
        P("dp", None),
        P("dp", "ctx"),
    )
    return jax.shard_map(
        shards,
        mesh=mesh,
        in_specs=placed,
        out_specs=(
            P("dp", "ctx", None),
            P("dp", "ctx", None),
            P("dp", "ctx", None),
            P("dp", "ctx", None),
        ),
        check_vma=False,
    )
```
